512 devices in a mesh: snap: 64 (over z, x), col: 8 (over y, core).
Axes of the slice: x: 4, y: 4, z: 16, core: 2. Of those that a mesh axis runs over, the one named last changes fastest.
Arguments:
- anomalies: bfloat16 [32768, 32768], P('snap', 'col'), may hold values from -16 to 16
- sketch_code: int32 [32768], P('col'), may hold values from 0 to 255
Outputs:
- scores: float32 [32768, 128], P('snap')
- eofs: float32 [32768, 128], P(('col', 'snap'))
The draws below stay inside these ranges and needn't reach their ends.
All inputs are finite; a program needn't handle non-finite values.
Results may differ from the reference program's by a relative error of at most 0.0026.
Values may be sent and summed in bfloat16 or wider, within the bound.
A program may use at most 64 MiB of HBM per device.

```python
import jax
import jax.numpy as jnp
from jax import lax

COLS = 32768
RANK = 128
SNAPS = 32768


def set_ends(drawn, stream_key, least, high):
    dims = drawn.shape
    index_at = [jax.random.randint(jax.random.fold_in(stream_key, axis), (), 0, dims[axis]) for axis in range(len(dims))]
    drawn = drawn.at[tuple(index_at)].set(least)
    longest = dims.index(max(dims))
    index_at[longest] = (index_at[longest] + 1) % dims[longest]
    return drawn.at[tuple(index_at)].set(high)


def strengthened(drawn, stream_key, source, target, shards_of, factor):
    owner, partner = [(jnp.arange(drawn.shape[axis_at]) // (drawn.shape[axis_at] // shards_of)).reshape([-1 if axis == axis_at else 1 for axis in range(drawn.ndim)]) for axis_at in (source, target)]
    chosen = jax.random.permutation(stream_key, shards_of)[partner]
    strong = (owner == chosen) | (owner == (partner + shards_of // 2) % shards_of)
    return jnp.where(strong, factor * drawn, drawn)


def block_levels(key, shape, shards, low, high):
    gain = 1.0
    for dim, parts in shards:
        draws = jax.random.uniform(jax.random.fold_in(jax.random.fold_in(key, 6), dim), (parts,), jnp.float32, low / len(shards), high / len(shards))
        gain = gain * jnp.repeat(jnp.exp(draws), shape[dim] // parts).reshape((-1,) + (1,) * (len(shape) - 1 - dim))
    return gain


def bell_draw_with(rng, extent, spread, reach, shards, heavy, held_as=jnp.bfloat16):
    result = spread * jax.random.normal(rng, extent, jnp.float32)
    if shards:
        result = result * block_levels(rng, extent, shards, -0.22, 0.18)
    return jnp.clip(strengthened(result, jax.random.fold_in(rng, 3), *heavy), -reach, reach).astype(held_as)


def setup_inputs(seed: int = 0) -> dict:
    key_list = jax.random.split(jax.random.key(seed), 3)
    anomalies = bell_draw_with(key_list[0], (SNAPS, COLS), 1.0, 16.0, ((0, 64), (1, 8)), (0, 1, 64, 4.0))
    sketch_code = set_ends(jax.random.randint(key_list[1], (COLS,), 0, 2 * RANK), jax.random.fold_in(key_list[1], 1), 0, (2 * RANK) - 1).astype(jnp.int32)
    return dict(anomalies=anomalies, sketch_code=sketch_code)


def sign_table(code, width):
    bucket = code % width
    sign = 1 - 2 * (code // width)
    hits = bucket[:, None] == jnp.arange(width, dtype=jnp.int32)[None, :]
    return jnp.where(hits, sign[:, None], 0).astype(jnp.bfloat16)

def reference(anomalies, sketch_code):
    omega = sign_table(sketch_code, RANK)
    sketch = jnp.dot(anomalies.astype(jnp.float32), omega.astype(jnp.float32), preferred_element_type=jnp.float32).astype(jnp.bfloat16)
    range_basis = lax.dot_general(anomalies.astype(jnp.float32), sketch.astype(jnp.float32), (((0,), (0,)), ((), ())), preferred_element_type=jnp.float32)
    gram = jnp.dot(range_basis.T, range_basis, precision=lax.Precision.HIGHEST)
    lower = jnp.linalg.cholesky(gram)
    eofs = lax.linalg.triangular_solve(lower, range_basis, left_side=False, lower=True, transpose_a=True)
    scores = jnp.dot(anomalies.astype(jnp.float32), eofs.astype(jnp.bfloat16).astype(jnp.float32), preferred_element_type=jnp.float32)
    return (scores, eofs)
```

```python
import functools

import jax
import jax.numpy as jnp
from jax import lax
from jax.experimental import pallas as pl
from jax.experimental.pallas import tpu as pltpu
from jax.sharding import PartitionSpec as P

RANK = 128
NX, NY, NZ, NC = 4, 4, 16, 2
NCOL = NY * NC
PLANE = NX * NCOL
ROWS = 64
TILE = NX * ROWS
LAG = 6
PANEL = 32
F32 = jnp.float32
HIGHEST = lax.Precision.HIGHEST
MESH = pl.DeviceIdType.MESH


def encode(value):
    top = jnp.maximum(jnp.max(jnp.abs(value), axis=0, keepdims=True), 1e-30)
    code = jnp.round(value * (32767.0 / top)).astype(jnp.int32).astype(jnp.int16)
    return code, top


def decode(code, top):
    return code.astype(jnp.int32).astype(F32) * (top * (1.0 / 32767.0))


def z_offset(j):
    return NZ // 2 + (1 - 2 * (j % 2)) * ((j + 1) // 2)


def factor_panel(m_ref, p):
    at = pl.multiple_of(p * PANEL, PANEL)
    g, e = m_ref[pl.ds(at, PANEL), :RANK], m_ref[pl.ds(at, PANEL), RANK:]
    g = pltpu.roll(g, lax.rem(RANK - at, RANK), 1)
    sub = lax.broadcasted_iota(jnp.int32, (PANEL, RANK), 0)
    lane = lax.broadcasted_iota(jnp.int32, (PANEL, RANK), 1)
    for j in range(0, PANEL, 2):
        c0 = jnp.broadcast_to(g[:, j : j + 1], (PANEL, RANK))
        c1 = jnp.broadcast_to(g[:, j + 1 : j + 2], (PANEL, RANK))
        a, b, d = c0[j : j + 1, :], c0[j + 1 : j + 2, :], c1[j + 1 : j + 2, :]
        b_over_a = b / a
        rest = d - b * b_over_a
        f1 = (c1 - c0 * b_over_a) / rest
        f0 = c0 / a - f1 * b_over_a
        below = sub > j + 1
        f0 = jnp.where(below, f0, jnp.where(sub == j + 1, b_over_a, 0.0))
        f1 = jnp.where(below, f1, 0.0)
        g, e = (
            g - f0 * g[j : j + 1, :] - f1 * g[j + 1 : j + 2, :],
            e - f0 * e[j : j + 1, :] - f1 * e[j + 1 : j + 2, :],
        )
    pivots = jnp.sum(jnp.where(sub == lane, g, 0.0), axis=1, keepdims=True)
    scale = lax.rsqrt(pivots)
    w, e = pltpu.roll(g * scale, at, 1), e * scale
    both = jnp.concatenate([w, e], axis=1)
    m_ref[pl.ds(at, PANEL), :] = both
    below = jnp.where(lane >= at + PANEL, w, 0.0)
    m_ref[...] -= lax.dot_general(below, both, (((0,), (0,)), ((), ())), precision=HIGHEST, preferred_element_type=F32)


def kernel(
    code_ref, a_hbm, scores_ref, eofs_ref,
    a, omega, half, core_in, y_in, sketch, sketch_t, tile,
    x_out, x_out_top, x_in, x_in_top, x_own,
    z_out, z_out_top, z_in, z_in_top, basis,
    all_code, all_top,
    gram_out, gram_in, gram_z, gram_all, system,
    proj, proj_sum, proj_in, proj_all,
    a_sem, core_sem, y_sem, s_sem,
    x_sem, x_top_sem, z_sem, z_top_sem,
    gz_sem, gz_top_sem, gx_sem, gx_top_sem,
    g1_sem, g2_sem, g3_sem, p1_sem, p2_sem,
):
    snap, col = lax.axis_index("snap"), lax.axis_index("col")
    z, x = snap // NX, snap % NX
    y, core = col // NC, col % NC
    place = x * NCOL + col

    def at_z(off):
        return {"snap": lax.rem(z + off, NZ) * NX + x, "col": col}

    def at_x(d):
        return {"snap": z * NX + lax.rem(x + d, NX), "col": col}

    def at_y(d):
        return {"snap": snap, "col": lax.rem(y + d, NY) * NC + core}

    def at_col(d):
        return {"snap": snap, "col": lax.rem(col + d, NCOL)}

    def at_plane(e):
        other = lax.rem(place + e, PLANE)
        return {"snap": z * NX + other // NCOL, "col": other % NCOL}

    other_core = {"snap": snap, "col": y * NC + (1 - core)}

    def remote(src, dst, sem, device):
        return pltpu.make_async_remote_copy(
            src_ref=src, dst_ref=dst, send_sem=sem[0], recv_sem=sem[1], device_id=device, device_id_type=MESH
        )

    def sems(ref, *index):
        return ref.at[(0, *index)], ref.at[(1, *index)]

    barrier = pltpu.get_barrier_semaphore()

    @pl.loop(1, PLANE)
    def _(e):
        pl.semaphore_signal(barrier, inc=1, device_id=at_plane(e), device_id_type=MESH)

    @pl.loop(1, NZ)
    def _(d):
        pl.semaphore_signal(barrier, inc=1, device_id=at_z(d), device_id_type=MESH)

    snaps = a.shape[0]
    kept = snaps // NC
    ranges = [pl.ds(pl.multiple_of((1 - core) * kept, kept), kept), pl.ds(pl.multiple_of(core * kept, kept), kept)]
    loads = [pltpu.make_async_copy(a_hbm.at[r], a.at[r], a_sem.at[i]) for i, r in enumerate(ranges)]
    for load in loads:
        load.start()

    width = 512

    @pl.loop(0, omega.shape[1] // width)
    def _(i):
        at = pl.ds(pl.multiple_of(i * width, width), width)
        code = code_ref[:, at]
        hits = lax.broadcasted_iota(jnp.int32, (RANK, width), 0) == code % RANK
        omega[:, at] = jnp.where(hits, jnp.where(code >= RANK, -1.0, 1.0), 0.0).astype(jnp.bfloat16)

    def sketch_rows(r):
        return lax.dot_general(a[r], omega[...], (((1,), (1,)), ((), ())), preferred_element_type=F32)

    loads[0].wait()
    half[0] = sketch_rows(ranges[0])
    pl.semaphore_wait(barrier, PLANE - 1 + NZ - 1)
    to_core = remote(half.at[0], core_in, sems(core_sem), other_core)
    to_core.start()
    loads[1].wait()
    mine = sketch_rows(ranges[1])
    to_core.wait()
    half[1] = mine + core_in[...]

    to_y = []
    for d in range(1, NY):
        rows = pl.ds(pl.multiple_of(lax.rem(y + d, NY) * ROWS, ROWS), ROWS)
        to_y.append(remote(half.at[1, rows], y_in.at[d - 1], sems(y_sem, d - 1), at_y(d)))
        to_y[-1].start()
    total = half[1, pl.ds(pl.multiple_of(y * ROWS, ROWS), ROWS), :]
    for d in range(1, NY):
        to_y[d - 1].wait_recv()
        total += y_in[d - 1]
    my_rows = pl.ds(pl.multiple_of(core * kept + y * ROWS, ROWS), ROWS)
    sketch[my_rows, :] = total.astype(jnp.bfloat16)
    for d in range(1, NCOL):
        remote(sketch.at[my_rows], sketch.at[my_rows], sems(s_sem, d - 1), at_col(d)).start()
    for copy in to_y:
        copy.wait_send()
    for d in range(1, NCOL):
        owner = lax.rem(col - d + NCOL, NCOL)
        rows = pl.ds(pl.multiple_of((owner % NC) * kept + (owner // NC) * ROWS, ROWS), ROWS)
        remote(sketch.at[rows], sketch.at[rows], sems(s_sem, d - 1), at_col(d)).wait()
    sketch_t[...] = sketch[...].astype(F32).T.astype(jnp.bfloat16)

    def x_copies(j, d):
        return (
            remote(x_out.at[j, d - 1], x_in.at[j, d - 1], sems(x_sem, j, d - 1), at_x(d)),
            remote(x_out_top.at[j, d - 1], x_in_top.at[j, d - 1], sems(x_top_sem, j, d - 1), at_x(d)),
        )

    def z_copies(j):
        return (
            remote(z_out.at[j], z_in.at[j], sems(z_sem, j), at_z(z_offset(j))),
            remote(z_out_top.at[j], z_in_top.at[j], sems(z_top_sem, j), at_z(z_offset(j))),
        )

    def tile_at(owner):
        return pl.ds(pl.multiple_of(owner * TILE, TILE), TILE)

    def produce(j):
        owner = lax.rem(z + z_offset(j), NZ)
        tile[...] = jnp.dot(sketch_t[...], a[:, tile_at(owner)], preferred_element_type=F32).T
        for d in range(1, NX):
            rows = pl.ds(pl.multiple_of(lax.rem(x + d, NX) * ROWS, ROWS), ROWS)
            x_out[j, d - 1], x_out_top[j, d - 1] = encode(tile[rows, :])
            for copy in x_copies(j, d):
                copy.start()
        x_own[j] = tile[pl.ds(pl.multiple_of(x * ROWS, ROWS), ROWS), :]

    def x_sum(j):
        total = x_own[j]
        for d in range(1, NX):
            for copy in x_copies(j, d):
                copy.wait()
            total += decode(x_in[j, d - 1], x_in_top[j, d - 1])
        return total

    def consume(j):
        z_out[j], z_out_top[j] = encode(x_sum(j))
        for copy in z_copies(j):
            copy.start()

    pl.loop(0, LAG)(produce)

    @pl.loop(LAG, NZ)
    def _(j):
        produce(j)
        consume(j - LAG)

    pl.loop(NZ - LAG, NZ - 1)(consume)
    basis[...] = x_sum(NZ - 1)

    @pl.loop(0, NZ - 1)
    def _(j):
        for copy in z_copies(j):
            copy.wait()
        basis[...] += decode(z_in[j], z_in_top[j])

    own = basis[...]
    gram = lax.dot_general(own, own, (((0,), (0,)), ((), ())), precision=HIGHEST, preferred_element_type=F32)
    for i in range(PLANE):
        gram_out[i] = gram[i * (RANK // PLANE) : (i + 1) * (RANK // PLANE), :]

    def g1_copy(e):
        return remote(gram_out.at[lax.rem(place + e, PLANE)], gram_in.at[e], sems(g1_sem, e), at_plane(e))

    @pl.loop(1, PLANE)
    def _(e):
        g1_copy(e).start()

    all_code[z, x], all_top[z, x] = encode(own)

    def gz_copies(owner, j):
        return (
            remote(all_code.at[owner, x], all_code.at[owner, x], sems(gz_sem, j), at_z(z_offset(j))),
            remote(all_top.at[owner, x], all_top.at[owner, x], sems(gz_top_sem, j), at_z(z_offset(j))),
        )

    def gx_copies(owner, j, d, source):
        return (
            remote(all_code.at[owner, source], all_code.at[owner, source], sems(gx_sem, j, d - 1), at_x(d)),
            remote(all_top.at[owner, source], all_top.at[owner, source], sems(gx_top_sem, j, d - 1), at_x(d)),
        )

    @pl.loop(0, NZ - 1)
    def _(j):
        for copy in gz_copies(z, j):
            copy.start()

    def forward(j):
        for d in range(1, NX):
            for copy in gx_copies(lax.rem(z - z_offset(j) + NZ, NZ), j, d, x):
                copy.start()

    def receive_and_forward(i):
        j = NZ - 2 - i
        for copy in gz_copies(lax.rem(z - z_offset(j) + NZ, NZ), j):
            copy.wait_recv()
        forward(j)

    forward(NZ - 1)

    gram_z[z] = gram_out[place]

    @pl.loop(1, PLANE)
    def _(e):
        g1_copy(e).wait_recv()
        gram_z[z] += gram_in[e]

    def g2_copy(owner, d):
        return remote(gram_z.at[owner], gram_z.at[owner], sems(g2_sem, d), at_z(d))

    @pl.loop(1, NZ)
    def _(d):
        g2_copy(z, d).start()

    pl.loop(0, NZ // 2)(receive_and_forward)

    @pl.loop(1, NZ)
    def _(d):
        g2_copy(lax.rem(z - d + NZ, NZ), d).wait_recv()

    gram_all[place] = jnp.sum(gram_z[...], axis=0)

    def g3_copy(owner, e):
        return remote(gram_all.at[owner], gram_all.at[owner], sems(g3_sem, e), at_plane(e))

    @pl.loop(1, PLANE)
    def _(e):
        g3_copy(place, e).start()

    pl.loop(NZ // 2, NZ - 1)(receive_and_forward)

    proj[...] = jnp.zeros_like(proj)

    @pl.loop(0, NZ)
    def _(i):
        j = NZ - 1 - i
        owner = lax.rem(z - z_offset(j) + NZ, NZ)
        for d in range(1, NX):
            for copy in gx_copies(owner, j, d, lax.rem(x - d + NX, NX)):
                copy.wait_recv()
        parts = [decode(all_code[owner, s], all_top[owner, s]) for s in range(NX)]
        value = jnp.concatenate(parts, axis=0)
        high = value.astype(jnp.bfloat16)
        low = (value - high.astype(F32)).astype(jnp.bfloat16)
        proj[...] += jnp.dot(
            a[:, tile_at(owner)], jnp.concatenate([high, low], axis=1), preferred_element_type=F32
        )

    def p1_copy(d):
        other = lax.rem(col + d, NCOL)
        rows = pl.ds(pl.multiple_of(other * ROWS, ROWS), ROWS)
        return remote(proj_sum.at[rows], proj_in.at[d - 1], sems(p1_sem, d - 1), at_col(d))

    proj_sum[...] = proj[:, :RANK] + proj[:, RANK:]
    for d in range(1, NCOL):
        p1_copy(d).start()

    @pl.loop(1, PLANE)
    def _(e):
        g3_copy(lax.rem(place - e + PLANE, PLANE), e).wait_recv()

    step = RANK // PLANE
    for i in range(PLANE):
        system[i * step : (i + 1) * step, :RANK] = gram_all[i]
    square = (RANK, RANK)
    system[:, RANK:] = jnp.where(
        lax.broadcasted_iota(jnp.int32, square, 0) == lax.broadcasted_iota(jnp.int32, square, 1), 1.0, 0.0
    )
    panels = RANK // PANEL
    pl.loop(0, panels // 2)(functools.partial(factor_panel, system))

    my_block = pl.ds(pl.multiple_of(col * ROWS, ROWS), ROWS)
    total = proj_sum[my_block, :]
    for d in range(1, NCOL):
        p1_copy(d).wait()
        total += proj_in[d - 1]
    proj_all[my_block, :] = total

    def p2_copy(d, owner):
        rows = pl.ds(pl.multiple_of(owner * ROWS, ROWS), ROWS)
        return remote(proj_all.at[rows], proj_all.at[rows], sems(p2_sem, d - 1), at_col(d))

    for d in range(1, NCOL):
        p2_copy(d, col).start()

    pl.loop(panels // 2, panels)(functools.partial(factor_panel, system))

    def whiten(value):
        return lax.dot_general(
            value, system[:, RANK:], (((1,), (1,)), ((), ())), precision=HIGHEST, preferred_element_type=F32
        )

    eofs_ref[...] = whiten(basis[...])
    for d in range(1, NCOL):
        p2_copy(d, lax.rem(col - d + NCOL, NCOL)).wait()
    scores_ref[...] = whiten(proj_all[...])

    @pl.loop(1, PLANE)
    def _(e):
        g1_copy(e).wait_send()
        g3_copy(place, e).wait_send()

    @pl.loop(1, NZ)
    def _(d):
        g2_copy(z, d).wait_send()

    @pl.loop(0, NZ - 1)
    def _(j):
        for copy in gz_copies(z, j):
            copy.wait_send()

    @pl.loop(0, NZ)
    def _(j):
        for d in range(1, NX):
            for copy in gx_copies(lax.rem(z - z_offset(j) + NZ, NZ), j, d, x):
                copy.wait_send()


def per_device(anomalies, sketch_code):
    snaps, cols = anomalies.shape
    vmem, dma = pltpu.VMEM, lambda *shape: pltpu.SemaphoreType.DMA((2, *shape))
    i16, bf16 = jnp.int16, jnp.bfloat16
    piece, top = (ROWS, RANK), (1, RANK)
    share = (RANK // PLANE, RANK)
    scratch = [
        vmem((snaps, cols), bf16),
        vmem((RANK, cols), bf16),
        vmem((2, snaps // NC, RANK), F32),
        vmem((snaps // NC, RANK), F32),
        vmem((NY - 1, *piece), F32),
        vmem((snaps, RANK), bf16),
        vmem((RANK, snaps), bf16),
        vmem((TILE, RANK), F32),
        vmem((NZ, NX - 1, *piece), i16),
        vmem((NZ, NX - 1, *top), F32),
        vmem((NZ, NX - 1, *piece), i16),
        vmem((NZ, NX - 1, *top), F32),
        vmem((NZ, *piece), F32),
        vmem((NZ - 1, *piece), i16),
        vmem((NZ - 1, *top), F32),
        vmem((NZ - 1, *piece), i16),
        vmem((NZ - 1, *top), F32),
        vmem(piece, F32),
        vmem((NZ, NX, *piece), i16),
        vmem((NZ, NX, *top), F32),
        vmem((PLANE, *share), F32),
        vmem((PLANE, *share), F32),
        vmem((NZ, *share), F32),
        vmem((PLANE, *share), F32),
        vmem((RANK, 2 * RANK), F32),
        vmem((snaps, 2 * RANK), F32),
        vmem((snaps, RANK), F32),
        vmem((NCOL - 1, *piece), F32),
        vmem((snaps, RANK), F32),
        pltpu.SemaphoreType.DMA((2,)),
        dma(),
        dma(NY - 1),
        dma(NCOL - 1),
        dma(NZ, NX - 1), dma(NZ, NX - 1),
        dma(NZ - 1), dma(NZ - 1),
        dma(NZ - 1), dma(NZ - 1),
        dma(NZ, NX - 1), dma(NZ, NX - 1),
        dma(PLANE), dma(NZ), dma(PLANE),
        dma(NCOL - 1), dma(NCOL - 1),
    ]
    return pl.pallas_call(
        kernel,
        out_shape=(jax.ShapeDtypeStruct((snaps, RANK), F32), jax.ShapeDtypeStruct(piece, F32)),
        in_specs=[pl.BlockSpec(memory_space=pltpu.VMEM), pl.BlockSpec(memory_space=pl.ANY)],
        out_specs=(pl.BlockSpec(memory_space=pltpu.VMEM), pl.BlockSpec(memory_space=pltpu.VMEM)),
        scratch_shapes=scratch,
        compiler_params=pltpu.CompilerParams(collective_id=0, has_side_effects=True, vmem_limit_bytes=48 << 20),
    )(sketch_code.reshape(1, cols), anomalies)


def solution(mesh):
    return jax.shard_map(
        per_device,
        mesh=mesh,
        in_specs=(P("snap", "col"), P("col")),
        out_specs=(P("snap", None), P(("col", "snap"), None)),
        check_vma=False,
    )
```

```python
import functools

import jax
import jax.numpy as jnp
from jax import lax
from jax.experimental import pallas as pl
from jax.experimental.pallas import tpu as pltpu
from jax.sharding import PartitionSpec as P

RANK = 128
NX, NY, NZ, NC = 4, 4, 16, 2
NCOL = NY * NC
PLANE = NX * NCOL
ROWS = 64
TILE = NX * ROWS
LAG = 6
GROUP = 4
PANEL = 32
AHEAD = 8
F32 = jnp.float32
HIGHEST = lax.Precision.HIGHEST
MESH = pl.DeviceIdType.MESH
DIRECT, RELAYS, NEAR = (6, 10, 3, 13, 8, 1, 15), (3, 13, 6, 10), (1, 15)

(S_CORE, S_Y, S_Y_TOP, S_BACK, R_X, R_X_TOP, R_Z, R_Z_TOP, G_Z, G_Z_TOP, G_X, G_X_TOP,
 GRAM_PLANE, GRAM_Z, GRAM_BACK, P_CORE, P_Y, P_Y_TOP, P_BACK) = range(19)
GROUPS = 19


def encode(value):
    top = jnp.maximum(jnp.max(jnp.abs(value), axis=0, keepdims=True), 1e-30)
    code = jnp.round(value * (32767.0 / top)).astype(jnp.int32).astype(jnp.int16)
    return code, top


def decode(code, top):
    return code.astype(jnp.int32).astype(F32) * (top * (1.0 / 32767.0))


def z_offset(j):
    return NZ // 2 + (1 - 2 * (j % 2)) * ((j + 1) // 2)


def factor_panel(m_ref, p):
    at = pl.multiple_of(p * PANEL, PANEL)
    g, e = m_ref[pl.ds(at, PANEL), :RANK], m_ref[pl.ds(at, PANEL), RANK:]
    g = pltpu.roll(g, lax.rem(RANK - at, RANK), 1)
    sub = lax.broadcasted_iota(jnp.int32, (PANEL, RANK), 0)
    lane = lax.broadcasted_iota(jnp.int32, (PANEL, RANK), 1)
    scale = jnp.zeros((PANEL, RANK), F32)
    for j in range(0, PANEL, AHEAD):
        columns = [jnp.broadcast_to(g[:, j + k : j + k + 1], (PANEL, RANK)) for k in range(AHEAD)]
        for k in range(AHEAD):
            row = j + k
            pivot = columns[k][row : row + 1, :]
            scale = jnp.where(sub == row, lax.rsqrt(pivot), scale)
            factor = jnp.where(sub > row, columns[k] * (1.0 / pivot), 0.0)
            for later in range(k + 1, AHEAD):
                columns[later] -= factor * columns[later][row : row + 1, :]
            g -= factor * g[row : row + 1, :]
            e -= factor * e[row : row + 1, :]
    w, e = pltpu.roll(g * scale, at, 1), e * scale
    both = jnp.concatenate([w, e], axis=1)
    m_ref[pl.ds(at, PANEL), :] = both
    below = jnp.where(lane >= at + PANEL, w, 0.0)
    m_ref[...] -= lax.dot_general(below, both, (((0,), (0,)), ((), ())), precision=HIGHEST, preferred_element_type=F32)


def kernel(
    code_hbm, a_hbm, scores_ref, eofs_ref,
    code_ref, a, omega, half, core_in, y_code, y_top, sketch, sketch_t, tile,
    x_out, x_out_top, x_in, x_in_top, x_own,
    z_out, z_out_top, z_in, z_in_top, basis,
    all_code, all_top,
    gram_out, gram_in, gram_z, gram_all, system,
    split, proj, proj_half, proj_in, proj_code, proj_top, proj_all,
    load_sem, send, recv, x_sem, x_top_sem, gz_sem, gx_sem,
):
    snap, col = lax.axis_index("snap"), lax.axis_index("col")
    z, x = snap // NX, snap % NX
    y, core = col // NC, col % NC
    place = x * NCOL + col

    def at_z(off):
        return {"snap": lax.rem(z + off, NZ) * NX + x, "col": col}

    def at_x(d):
        return {"snap": z * NX + lax.rem(x + d, NX), "col": col}

    def at_y(d):
        return {"snap": snap, "col": lax.rem(y + d, NY) * NC + core}

    def at_plane(e):
        other = lax.rem(place + e, PLANE)
        return {"snap": z * NX + other // NCOL, "col": other % NCOL}

    other_core = {"snap": snap, "col": y * NC + (1 - core)}

    def remote(src, dst, group, device, recv_sem=None):
        return pltpu.make_async_remote_copy(
            src_ref=src,
            dst_ref=dst,
            send_sem=send.at[group],
            recv_sem=recv.at[group] if recv_sem is None else recv_sem,
            device_id=device,
            device_id_type=MESH,
        )

    def wait_recv(region, group, recv_sem=None):
        remote(region, region, group, other_core, recv_sem).wait_recv()

    def wait_send(region, group):
        remote(region, region, group, other_core).wait_send()

    barrier = pltpu.get_barrier_semaphore()

    snaps = a.shape[0]
    kept = snaps // NC
    other_rows = pl.ds(pl.multiple_of((1 - core) * kept, kept), kept)
    core_rows = pl.ds(pl.multiple_of(core * kept, kept), kept)
    loads = [pltpu.make_async_copy(code_hbm, code_ref, load_sem.at[0])]
    loads += [pltpu.make_async_copy(a_hbm.at[r], a.at[r], load_sem.at[1 + i]) for i, r in enumerate((other_rows, core_rows))]
    for load in loads:
        load.start()

    @pl.loop(1, PLANE)
    def _(e):
        pl.semaphore_signal(barrier, inc=1, device_id=at_plane(e), device_id_type=MESH)

    @pl.loop(1, NZ)
    def _(d):
        pl.semaphore_signal(barrier, inc=1, device_id=at_z(d), device_id_type=MESH)

    width = 512
    loads[0].wait()

    @pl.loop(0, omega.shape[1] // width)
    def _(i):
        at = pl.ds(pl.multiple_of(i * width, width), width)
        code = code_ref[:, at]
        hits = lax.broadcasted_iota(jnp.int32, (RANK, width), 0) == code % RANK
        omega[:, at] = jnp.where(hits, jnp.where(code >= RANK, -1.0, 1.0), 0.0).astype(jnp.bfloat16)

    def sketch_rows(r):
        return lax.dot_general(a[r], omega[...], (((1,), (1,)), ((), ())), preferred_element_type=F32)

    loads[1].wait()
    half[...] = sketch_rows(other_rows)
    pl.semaphore_wait(barrier, PLANE - 1 + NZ - 1)
    to_core = remote(half, core_in, S_CORE, other_core)
    to_core.start()
    loads[2].wait()
    mine = sketch_rows(core_rows)

    def sum_over_y(value, code_buffer, top_buffer, group):
        code_buffer[y], top_buffer[y] = encode(value)
        for d in range(1, NY):
            remote(code_buffer.at[y], code_buffer.at[y], group, at_y(d)).start()
            remote(top_buffer.at[y], top_buffer.at[y], group + 1, at_y(d)).start()

    def summed_over_y(code_buffer, top_buffer, group):
        for k, buffer in enumerate((code_buffer, top_buffer)):
            wait_recv(buffer.at[pl.ds(0, NY - 1)], group + k)
            wait_send(buffer.at[pl.ds(0, NY - 1)], group + k)
        return sum(decode(code_buffer[i], top_buffer[i]) for i in range(NY))

    to_core.wait_recv()
    sum_over_y(mine + core_in[...], y_code, y_top, S_Y)
    to_core.wait_send()
    sketch[core_rows, :] = summed_over_y(y_code, y_top, S_Y).astype(jnp.bfloat16)
    remote(sketch.at[core_rows], sketch.at[core_rows], S_BACK, other_core).start()
    wait_recv(sketch.at[other_rows], S_BACK)
    sketch_t[...] = sketch[...].astype(F32).T.astype(jnp.bfloat16)
    wait_send(sketch.at[core_rows], S_BACK)

    def z_copies(j):
        return (
            remote(z_out.at[j], z_in.at[j], R_Z, at_z(z_offset(j))),
            remote(z_out_top.at[j], z_in_top.at[j], R_Z_TOP, at_z(z_offset(j))),
        )

    def tile_at(owner):
        return pl.ds(pl.multiple_of(owner * TILE, TILE), TILE)

    def produce(j):
        owner = lax.rem(z + z_offset(j), NZ)
        tile[...] = jnp.dot(sketch_t[...], a[:, tile_at(owner)], preferred_element_type=F32).T
        for d in range(1, NX):
            rows = pl.ds(pl.multiple_of(lax.rem(x + d, NX) * ROWS, ROWS), ROWS)
            x_out[j, d - 1], x_out_top[j, d - 1] = encode(tile[rows, :])
            remote(x_out.at[j, d - 1], x_in.at[j, d - 1], R_X, at_x(d), x_sem.at[j]).start()
            remote(x_out_top.at[j, d - 1], x_in_top.at[j, d - 1], R_X_TOP, at_x(d), x_top_sem.at[j]).start()
        x_own[j] = tile[pl.ds(pl.multiple_of(x * ROWS, ROWS), ROWS), :]

    def x_sum(j):
        wait_recv(x_in.at[j], R_X, x_sem.at[j])
        wait_recv(x_in_top.at[j], R_X_TOP, x_top_sem.at[j])
        total = x_own[j]
        for d in range(1, NX):
            total += decode(x_in[j, d - 1], x_in_top[j, d - 1])
        return total

    def consume(j):
        z_out[j], z_out_top[j] = encode(x_sum(j))
        for copy in z_copies(j):
            copy.start()

    pl.loop(0, LAG)(produce)

    @pl.loop(LAG, NZ)
    def _(j):
        produce(j)
        consume(j - LAG)

    pl.loop(NZ - LAG, NZ - 1)(consume)
    basis[...] = x_sum(NZ - 1)
    wait_recv(z_in, R_Z)
    wait_recv(z_in_top, R_Z_TOP)

    @pl.loop(0, NZ - 1)
    def _(j):
        basis[...] += decode(z_in[j], z_in_top[j])

    own = basis[...]
    all_code[z, x], all_top[x, z] = encode(own)

    def gather_z(offset, d):
        chunk = all_code.at[lax.rem(z - offset + NZ, NZ), x]
        remote(chunk, chunk, G_Z, at_z(d), gz_sem.at[(offset + d) % NZ]).start()

    def gather_x(offset):
        chunk = all_code.at[lax.rem(z - offset + NZ, NZ), x]
        for d in range(1, NX):
            remote(chunk, chunk, G_X, at_x(d), gx_sem.at[offset]).start()

    def arrived(offset):
        wait_recv(all_code.at[lax.rem(z - offset + NZ, NZ), x], G_Z, gz_sem.at[offset])

    for d in DIRECT:
        gather_z(0, d)

    @pl.loop(1, NZ)
    def _(d):
        remote(all_top.at[x, z], all_top.at[x, z], G_Z_TOP, at_z(d)).start()

    gather_x(0)

    gram = lax.dot_general(own, own, (((0,), (0,)), ((), ())), precision=HIGHEST, preferred_element_type=F32)
    share = RANK // PLANE
    for i in range(PLANE):
        gram_out[i] = gram[i * share : (i + 1) * share, :]

    @pl.loop(1, PLANE)
    def _(e):
        remote(gram_out.at[lax.rem(place + e, PLANE)], gram_in.at[e - 1], GRAM_PLANE, at_plane(e)).start()

    for offset in (1, 15):
        arrived(offset)
        gather_x(offset)

    def relay(offset):
        arrived(offset)
        for d in NEAR:
            gather_z(offset, d)
        gather_x(offset)

    for offset in RELAYS[:2]:
        relay(offset)

    wait_recv(gram_in, GRAM_PLANE)
    gram_z[z] = gram_out[place] + jnp.sum(gram_in[...], axis=0)

    @pl.loop(1, NZ)
    def _(d):
        remote(gram_z.at[z], gram_z.at[z], GRAM_Z, at_z(d)).start()

    for offset in RELAYS[2:]:
        relay(offset)
    for offset in (2, 4, 14, 12, 8):
        arrived(offset)
        gather_x(offset)
    wait_recv(all_top.at[0, pl.ds(0, NZ - 1)], G_Z_TOP)
    for d in range(1, NX):
        remote(all_top.at[x], all_top.at[x], G_X_TOP, at_x(d)).start()
    for offset in (5, 7, 11, 9):
        arrived(offset)
        gather_x(offset)

    wait_recv(gram_z.at[pl.ds(0, NZ - 1)], GRAM_Z)
    gram_all[place] = jnp.sum(gram_z[...], axis=0)

    @pl.loop(1, PLANE)
    def _(e):
        remote(gram_all.at[place], gram_all.at[place], GRAM_BACK, at_plane(e)).start()

    proj[...] = jnp.zeros_like(proj)
    wait_recv(all_top.at[pl.ds(0, NX - 1)], G_X_TOP)

    @pl.loop(0, NZ // GROUP)
    def _(i):
        first = lax.rem(z // GROUP + i, NZ // GROUP) * GROUP

        @pl.loop(0, GROUP)
        def _(t):
            owner = first + t
            wait_recv(all_code.at[owner, pl.ds(0, NX - 1)], G_X, gx_sem.at[lax.rem(z - owner + NZ, NZ)])
            for s in range(NX):
                value = decode(all_code[owner, s], all_top[s, owner])
                high = value.astype(jnp.bfloat16)
                rows = pl.ds(pl.multiple_of((t * NX + s) * ROWS, ROWS), ROWS)
                split[rows, :RANK] = high
                split[rows, RANK:] = (value - high.astype(F32)).astype(jnp.bfloat16)

        columns = pl.ds(pl.multiple_of(first * TILE, GROUP * TILE), GROUP * TILE)
        proj[...] += jnp.dot(a[:, columns], split[...], preferred_element_type=F32)

    proj_half[...] = proj[other_rows, :RANK] + proj[other_rows, RANK:]
    remote(proj_half, proj_in, P_CORE, other_core).start()
    mine = proj[core_rows, :RANK] + proj[core_rows, RANK:]
    wait_recv(proj_in, P_CORE)
    sum_over_y(mine + proj_in[...], proj_code, proj_top, P_Y)

    wait_recv(gram_all.at[pl.ds(0, PLANE - 1)], GRAM_BACK)
    for i in range(PLANE):
        system[i * share : (i + 1) * share, :RANK] = gram_all[i]
    square = (RANK, RANK)
    system[:, RANK:] = jnp.where(
        lax.broadcasted_iota(jnp.int32, square, 0) == lax.broadcasted_iota(jnp.int32, square, 1), 1.0, 0.0
    )
    panels = RANK // PANEL
    pl.loop(0, panels // 2)(functools.partial(factor_panel, system))

    proj_all[core_rows, :] = summed_over_y(proj_code, proj_top, P_Y)
    remote(proj_all.at[core_rows], proj_all.at[core_rows], P_BACK, other_core).start()

    pl.loop(panels // 2, panels)(functools.partial(factor_panel, system))

    def whiten(value):
        return lax.dot_general(
            value, system[:, RANK:], (((1,), (1,)), ((), ())), precision=HIGHEST, preferred_element_type=F32
        )

    eofs_ref[...] = whiten(basis[...])
    wait_recv(proj_all.at[other_rows], P_BACK)
    scores_ref[...] = whiten(proj_all[...])

    wait_send(x_out, R_X)
    wait_send(x_out_top, R_X_TOP)
    wait_send(z_out, R_Z)
    wait_send(z_out_top, R_Z_TOP)
    wait_send(z_in, G_Z)
    wait_send(x_in, G_X)
    wait_send(z_in_top, G_Z_TOP)
    wait_send(all_top.at[pl.ds(0, NX - 1)], G_X_TOP)
    wait_send(gram_in, GRAM_PLANE)
    wait_send(gram_z.at[pl.ds(0, NZ - 1)], GRAM_Z)
    wait_send(gram_in, GRAM_BACK)
    wait_send(proj_half, P_CORE)
    wait_send(proj_all.at[core_rows], P_BACK)


def per_device(anomalies, sketch_code):
    snaps, cols = anomalies.shape
    vmem, dma = pltpu.VMEM, lambda *shape: pltpu.SemaphoreType.DMA(shape)
    i16, bf16 = jnp.int16, jnp.bfloat16
    piece, top = (ROWS, RANK), (1, RANK)
    share = (RANK // PLANE, RANK)
    kept = (snaps // NC, RANK)
    scratch = [
        vmem((1, cols), jnp.int32),
        vmem((snaps, cols), bf16),
        vmem((RANK, cols), bf16),
        vmem(kept, F32),
        vmem(kept, F32),
        vmem((NY, *kept), i16),
        vmem((NY, *top), F32),
        vmem((snaps, RANK), bf16),
        vmem((RANK, snaps), bf16),
        vmem((TILE, RANK), F32),
        vmem((NZ, NX - 1, *piece), i16),
        vmem((NZ, NX - 1, *top), F32),
        vmem((NZ, NX - 1, *piece), i16),
        vmem((NZ, NX - 1, *top), F32),
        vmem((NZ, *piece), F32),
        vmem((NZ - 1, *piece), i16),
        vmem((NZ - 1, *top), F32),
        vmem((NZ - 1, *piece), i16),
        vmem((NZ - 1, *top), F32),
        vmem(piece, F32),
        vmem((NZ, NX, *piece), i16),
        vmem((NX, NZ, *top), F32),
        vmem((PLANE, *share), F32),
        vmem((PLANE - 1, *share), F32),
        vmem((NZ, *share), F32),
        vmem((PLANE, *share), F32),
        vmem((RANK, 2 * RANK), F32),
        vmem((GROUP * TILE, 2 * RANK), bf16),
        vmem((snaps, 2 * RANK), F32),
        vmem(kept, F32),
        vmem(kept, F32),
        vmem((NY, *kept), i16),
        vmem((NY, *top), F32),
        vmem((snaps, RANK), F32),
        dma(3), dma(GROUPS), dma(GROUPS),
        dma(NZ), dma(NZ), dma(NZ), dma(NZ),
    ]
    return pl.pallas_call(
        kernel,
        out_shape=(jax.ShapeDtypeStruct((snaps, RANK), F32), jax.ShapeDtypeStruct(piece, F32)),
        in_specs=[pl.BlockSpec(memory_space=pltpu.HBM)] * 2,
        out_specs=(pl.BlockSpec(memory_space=pltpu.VMEM), pl.BlockSpec(memory_space=pltpu.VMEM)),
        scratch_shapes=scratch,
        compiler_params=pltpu.CompilerParams(collective_id=0, has_side_effects=True, vmem_limit_bytes=48 << 20),
    )(sketch_code.reshape(1, cols), anomalies)


def solution(mesh):
    return jax.shard_map(
        per_device,
        mesh=mesh,
        in_specs=(P("snap", "col"), P("col")),
        out_specs=(P("snap", None), P(("col", "snap"), None)),
        check_vma=False,
    )
```

```python
import functools

import jax
import jax.numpy as jnp
from jax import lax
from jax.experimental import pallas as pl
from jax.experimental.pallas import tpu as pltpu
from jax.sharding import PartitionSpec as P

RANK = 128
NX, NY, NZ, NC = 4, 4, 16, 2
NCOL = NY * NC
PLANE = NX * NCOL
ROWS = 64
TILE = NX * ROWS
LAG = 6
GROUP = 4
PANEL = 32
AHEAD = 8
F32 = jnp.float32
HIGHEST = lax.Precision.HIGHEST
MESH = pl.DeviceIdType.MESH
DIRECT, RELAYS, NEAR = (1, 15, 8, 4, 12, 2), (4, 12, 8), (1, 15, 2)

(S_CORE, S_Y, S_Y_TOP, S_BACK, R_X, R_X_TOP, R_Z, R_Z_TOP, G_Z, G_Z_TOP, G_X, G_X_TOP,
 GRAM_PLANE, GRAM_Z, GRAM_BACK, P_CORE, P_Y, P_Y_TOP, P_BACK) = range(19)
GROUPS = 19


def encode(value):
    top = jnp.maximum(jnp.max(jnp.abs(value), axis=0, keepdims=True), 1e-30)
    code = jnp.round(value * (32767.0 / top)).astype(jnp.int32).astype(jnp.int16)
    return code, top


def decode(code, top):
    return code.astype(jnp.int32).astype(F32) * (top * (1.0 / 32767.0))


def z_offset(j):
    return NZ // 2 + (1 - 2 * (j % 2)) * ((j + 1) // 2)


def factor_panel(m_ref, p):
    at = pl.multiple_of(p * PANEL, PANEL)
    g, e = m_ref[pl.ds(at, PANEL), :RANK], m_ref[pl.ds(at, PANEL), RANK:]
    g = pltpu.roll(g, lax.rem(RANK - at, RANK), 1)
    sub = lax.broadcasted_iota(jnp.int32, (PANEL, RANK), 0)
    lane = lax.broadcasted_iota(jnp.int32, (PANEL, RANK), 1)
    scale = jnp.zeros((PANEL, RANK), F32)
    for j in range(0, PANEL, AHEAD):
        columns = [jnp.broadcast_to(g[:, j + k : j + k + 1], (PANEL, RANK)) for k in range(AHEAD)]
        for k in range(AHEAD):
            row = j + k
            pivot = columns[k][row : row + 1, :]
            scale = jnp.where(sub == row, lax.rsqrt(pivot), scale)
            factor = jnp.where(sub > row, columns[k] * (1.0 / pivot), 0.0)
            for later in range(k + 1, AHEAD):
                columns[later] -= factor * columns[later][row : row + 1, :]
            g -= factor * g[row : row + 1, :]
            e -= factor * e[row : row + 1, :]
    w, e = pltpu.roll(g * scale, at, 1), e * scale
    both = jnp.concatenate([w, e], axis=1)
    m_ref[pl.ds(at, PANEL), :] = both
    below = jnp.where(lane >= at + PANEL, w, 0.0)
    m_ref[...] -= lax.dot_general(below, both, (((0,), (0,)), ((), ())), precision=HIGHEST, preferred_element_type=F32)


def kernel(
    code_hbm, a_hbm, scores_ref, eofs_ref,
    code_ref, a, omega, half, core_in, y_code, y_top, sketch, sketch_t, tile,
    x_out, x_out_top, x_in, x_in_top, x_own,
    z_out, z_out_top, z_in, z_in_top, basis,
    all_code, all_top,
    gram_out, gram_in, gram_z, gram_all, system,
    split, proj, proj_half, proj_in, proj_code, proj_top, proj_all,
    load_sem, send, recv, x_sem, x_top_sem, gz_sem, gx_sem,
):
    snap, col = lax.axis_index("snap"), lax.axis_index("col")
    z, x = snap // NX, snap % NX
    y, core = col // NC, col % NC
    place = x * NCOL + col

    def at_z(off):
        return {"snap": lax.rem(z + off, NZ) * NX + x, "col": col}

    def at_x(d):
        return {"snap": z * NX + lax.rem(x + d, NX), "col": col}

    def at_y(d):
        return {"snap": snap, "col": lax.rem(y + d, NY) * NC + core}

    def at_plane(e):
        other = lax.rem(place + e, PLANE)
        return {"snap": z * NX + other // NCOL, "col": other % NCOL}

    other_core = {"snap": snap, "col": y * NC + (1 - core)}

    def remote(src, dst, group, device, recv_sem=None):
        return pltpu.make_async_remote_copy(
            src_ref=src,
            dst_ref=dst,
            send_sem=send.at[group],
            recv_sem=recv.at[group] if recv_sem is None else recv_sem,
            device_id=device,
            device_id_type=MESH,
        )

    def wait_recv(region, group, recv_sem=None):
        remote(region, region, group, other_core, recv_sem).wait_recv()

    def wait_send(region, group):
        remote(region, region, group, other_core).wait_send()

    barrier = pltpu.get_barrier_semaphore()

    snaps = a.shape[0]
    kept = snaps // NC
    other_rows = pl.ds(pl.multiple_of((1 - core) * kept, kept), kept)
    core_rows = pl.ds(pl.multiple_of(core * kept, kept), kept)
    loads = [pltpu.make_async_copy(code_hbm, code_ref, load_sem.at[0])]
    loads += [pltpu.make_async_copy(a_hbm.at[r], a.at[r], load_sem.at[1 + i]) for i, r in enumerate((other_rows, core_rows))]
    for load in loads:
        load.start()

    @pl.loop(1, PLANE)
    def _(e):
        pl.semaphore_signal(barrier, inc=1, device_id=at_plane(e), device_id_type=MESH)

    @pl.loop(1, NZ)
    def _(d):
        pl.semaphore_signal(barrier, inc=1, device_id=at_z(d), device_id_type=MESH)

    width = 512
    loads[0].wait()

    @pl.loop(0, omega.shape[1] // width)
    def _(i):
        at = pl.ds(pl.multiple_of(i * width, width), width)
        code = code_ref[:, at]
        hits = lax.broadcasted_iota(jnp.int32, (RANK, width), 0) == code % RANK
        omega[:, at] = jnp.where(hits, jnp.where(code >= RANK, -1.0, 1.0), 0.0).astype(jnp.bfloat16)

    def sketch_rows(r):
        return lax.dot_general(a[r], omega[...], (((1,), (1,)), ((), ())), preferred_element_type=F32)

    loads[1].wait()
    half[...] = sketch_rows(other_rows)
    pl.semaphore_wait(barrier, PLANE - 1 + NZ - 1)
    to_core = remote(half, core_in, S_CORE, other_core)
    to_core.start()
    loads[2].wait()
    mine = sketch_rows(core_rows)

    def sum_over_y(value, code_buffer, top_buffer, group):
        code_buffer[y], top_buffer[y] = encode(value)
        for d in range(1, NY):
            remote(code_buffer.at[y], code_buffer.at[y], group, at_y(d)).start()
            remote(top_buffer.at[y], top_buffer.at[y], group + 1, at_y(d)).start()

    def summed_over_y(code_buffer, top_buffer, group):
        for k, buffer in enumerate((code_buffer, top_buffer)):
            wait_recv(buffer.at[pl.ds(0, NY - 1)], group + k)
            wait_send(buffer.at[pl.ds(0, NY - 1)], group + k)
        return sum(decode(code_buffer[i], top_buffer[i]) for i in range(NY))

    to_core.wait_recv()
    sum_over_y(mine + core_in[...], y_code, y_top, S_Y)
    to_core.wait_send()
    sketch[core_rows, :] = summed_over_y(y_code, y_top, S_Y).astype(jnp.bfloat16)
    remote(sketch.at[core_rows], sketch.at[core_rows], S_BACK, other_core).start()
    wait_recv(sketch.at[other_rows], S_BACK)
    sketch_t[...] = sketch[...].astype(F32).T.astype(jnp.bfloat16)
    wait_send(sketch.at[core_rows], S_BACK)

    def z_copies(j):
        return (
            remote(z_out.at[j], z_in.at[j], R_Z, at_z(z_offset(j))),
            remote(z_out_top.at[j], z_in_top.at[j], R_Z_TOP, at_z(z_offset(j))),
        )

    def tile_at(owner):
        return pl.ds(pl.multiple_of(owner * TILE, TILE), TILE)

    def produce(j):
        owner = lax.rem(z + z_offset(j), NZ)
        tile[...] = jnp.dot(sketch_t[...], a[:, tile_at(owner)], preferred_element_type=F32).T
        for d in range(1, NX):
            rows = pl.ds(pl.multiple_of(lax.rem(x + d, NX) * ROWS, ROWS), ROWS)
            x_out[j, d - 1], x_out_top[j, d - 1] = encode(tile[rows, :])
            remote(x_out.at[j, d - 1], x_in.at[j, d - 1], R_X, at_x(d), x_sem.at[j]).start()
            remote(x_out_top.at[j, d - 1], x_in_top.at[j, d - 1], R_X_TOP, at_x(d), x_top_sem.at[j]).start()
        x_own[j] = tile[pl.ds(pl.multiple_of(x * ROWS, ROWS), ROWS), :]

    def x_sum(j):
        wait_recv(x_in.at[j], R_X, x_sem.at[j])
        wait_recv(x_in_top.at[j], R_X_TOP, x_top_sem.at[j])
        total = x_own[j]
        for d in range(1, NX):
            total += decode(x_in[j, d - 1], x_in_top[j, d - 1])
        return total

    def consume(j):
        z_out[j], z_out_top[j] = encode(x_sum(j))
        for copy in z_copies(j):
            copy.start()

    pl.loop(0, LAG)(produce)

    @pl.loop(LAG, NZ)
    def _(j):
        produce(j)
        consume(j - LAG)

    pl.loop(NZ - LAG, NZ - 1)(consume)
    basis[...] = x_sum(NZ - 1)
    wait_recv(z_in, R_Z)
    wait_recv(z_in_top, R_Z_TOP)

    @pl.loop(0, NZ - 1)
    def _(j):
        basis[...] += decode(z_in[j], z_in_top[j])

    own = basis[...]
    all_code[z, x], all_top[x, z] = encode(own)

    def gather_z(offset, d):
        chunk = all_code.at[lax.rem(z - offset + NZ, NZ), x]
        remote(chunk, chunk, G_Z, at_z(d), gz_sem.at[(offset + d) % NZ]).start()

    def gather_x(offset):
        chunk = all_code.at[lax.rem(z - offset + NZ, NZ), x]
        for d in range(1, NX):
            remote(chunk, chunk, G_X, at_x(d), gx_sem.at[offset]).start()

    def arrived(offset):
        wait_recv(all_code.at[lax.rem(z - offset + NZ, NZ), x], G_Z, gz_sem.at[offset])

    for d in DIRECT[:5]:
        gather_z(0, d)

    gram = lax.dot_general(own, own, (((0,), (0,)), ((), ())), precision=HIGHEST, preferred_element_type=F32)
    share = RANK // PLANE
    for i in range(PLANE):
        gram_out[i] = gram[i * share : (i + 1) * share, :]

    @pl.loop(1, PLANE)
    def _(e):
        remote(gram_out.at[lax.rem(place + e, PLANE)], gram_in.at[e - 1], GRAM_PLANE, at_plane(e)).start()

    for d in DIRECT[5:]:
        gather_z(0, d)

    @pl.loop(1, NZ)
    def _(d):
        remote(all_top.at[x, z], all_top.at[x, z], G_Z_TOP, at_z(d)).start()

    gather_x(0)

    for offset in (1, 15):
        arrived(offset)
        gather_x(offset)

    def relay(offset):
        arrived(offset)
        for d in NEAR:
            gather_z(offset, d)
        gather_x(offset)

    for offset in RELAYS[:2]:
        relay(offset)

    wait_recv(gram_in, GRAM_PLANE)
    gram_z[z] = gram_out[place] + jnp.sum(gram_in[...], axis=0)

    @pl.loop(1, NZ)
    def _(d):
        remote(gram_z.at[z], gram_z.at[z], GRAM_Z, at_z(d)).start()

    for offset in RELAYS[2:]:
        relay(offset)
    for offset in (2, 3, 5, 13, 11):
        arrived(offset)
        gather_x(offset)
    wait_recv(all_top.at[0, pl.ds(0, NZ - 1)], G_Z_TOP)
    for d in range(1, NX):
        remote(all_top.at[x], all_top.at[x], G_X_TOP, at_x(d)).start()
    for offset in (6, 14, 7, 9, 10):
        arrived(offset)
        gather_x(offset)

    wait_recv(gram_z.at[pl.ds(0, NZ - 1)], GRAM_Z)
    gram_all[place] = jnp.sum(gram_z[...], axis=0)

    @pl.loop(1, PLANE)
    def _(e):
        remote(gram_all.at[place], gram_all.at[place], GRAM_BACK, at_plane(e)).start()

    proj[...] = jnp.zeros_like(proj)
    wait_recv(all_top.at[pl.ds(0, NX - 1)], G_X_TOP)

    @pl.loop(0, NZ // GROUP)
    def _(i):
        first = lax.rem(z // GROUP + i, NZ // GROUP) * GROUP

        @pl.loop(0, GROUP)
        def _(t):
            owner = first + t
            wait_recv(all_code.at[owner, pl.ds(0, NX - 1)], G_X, gx_sem.at[lax.rem(z - owner + NZ, NZ)])
            for s in range(NX):
                value = decode(all_code[owner, s], all_top[s, owner])
                high = value.astype(jnp.bfloat16)
                rows = pl.ds(pl.multiple_of((t * NX + s) * ROWS, ROWS), ROWS)
                split[rows, :RANK] = high
                split[rows, RANK:] = (value - high.astype(F32)).astype(jnp.bfloat16)

        columns = pl.ds(pl.multiple_of(first * TILE, GROUP * TILE), GROUP * TILE)
        proj[...] += jnp.dot(a[:, columns], split[...], preferred_element_type=F32)

    proj_half[...] = proj[other_rows, :RANK] + proj[other_rows, RANK:]
    remote(proj_half, proj_in, P_CORE, other_core).start()
    mine = proj[core_rows, :RANK] + proj[core_rows, RANK:]
    wait_recv(proj_in, P_CORE)
    sum_over_y(mine + proj_in[...], proj_code, proj_top, P_Y)

    wait_recv(gram_all.at[pl.ds(0, PLANE - 1)], GRAM_BACK)
    for i in range(PLANE):
        system[i * share : (i + 1) * share, :RANK] = gram_all[i]
    square = (RANK, RANK)
    system[:, RANK:] = jnp.where(
        lax.broadcasted_iota(jnp.int32, square, 0) == lax.broadcasted_iota(jnp.int32, square, 1), 1.0, 0.0
    )
    pl.loop(0, RANK // PANEL)(functools.partial(factor_panel, system))

    proj_all[core_rows, :] = summed_over_y(proj_code, proj_top, P_Y)
    remote(proj_all.at[core_rows], proj_all.at[core_rows], P_BACK, other_core).start()

    def whiten(value):
        return lax.dot_general(
            value, system[:, RANK:], (((1,), (1,)), ((), ())), precision=HIGHEST, preferred_element_type=F32
        )

    scores_ref[core_rows, :] = whiten(proj_all[core_rows, :])
    eofs_ref[...] = whiten(basis[...])
    wait_recv(proj_all.at[other_rows], P_BACK)
    scores_ref[other_rows, :] = whiten(proj_all[other_rows, :])

    wait_send(x_out, R_X)
    wait_send(x_out_top, R_X_TOP)
    wait_send(z_out, R_Z)
    wait_send(z_out_top, R_Z_TOP)
    wait_send(z_in, G_Z)
    wait_send(x_in, G_X)
    wait_send(z_in_top, G_Z_TOP)
    wait_send(all_top.at[pl.ds(0, NX - 1)], G_X_TOP)
    wait_send(gram_in, GRAM_PLANE)
    wait_send(gram_z.at[pl.ds(0, NZ - 1)], GRAM_Z)
    wait_send(gram_in, GRAM_BACK)
    wait_send(proj_half, P_CORE)
    wait_send(proj_all.at[core_rows], P_BACK)


def per_device(anomalies, sketch_code):
    snaps, cols = anomalies.shape
    vmem, dma = pltpu.VMEM, lambda *shape: pltpu.SemaphoreType.DMA(shape)
    i16, bf16 = jnp.int16, jnp.bfloat16
    piece, top = (ROWS, RANK), (1, RANK)
    share = (RANK // PLANE, RANK)
    kept = (snaps // NC, RANK)
    scratch = [
        vmem((1, cols), jnp.int32),
        vmem((snaps, cols), bf16),
        vmem((RANK, cols), bf16),
        vmem(kept, F32),
        vmem(kept, F32),
        vmem((NY, *kept), i16),
        vmem((NY, *top), F32),
        vmem((snaps, RANK), bf16),
        vmem((RANK, snaps), bf16),
        vmem((TILE, RANK), F32),
        vmem((NZ, NX - 1, *piece), i16),
        vmem((NZ, NX - 1, *top), F32),
        vmem((NZ, NX - 1, *piece), i16),
        vmem((NZ, NX - 1, *top), F32),
        vmem((NZ, *piece), F32),
        vmem((NZ - 1, *piece), i16),
        vmem((NZ - 1, *top), F32),
        vmem((NZ - 1, *piece), i16),
        vmem((NZ - 1, *top), F32),
        vmem(piece, F32),
        vmem((NZ, NX, *piece), i16),
        vmem((NX, NZ, *top), F32),
        vmem((PLANE, *share), F32),
        vmem((PLANE - 1, *share), F32),
        vmem((NZ, *share), F32),
        vmem((PLANE, *share), F32),
        vmem((RANK, 2 * RANK), F32),
        vmem((GROUP * TILE, 2 * RANK), bf16),
        vmem((snaps, 2 * RANK), F32),
        vmem(kept, F32),
        vmem(kept, F32),
        vmem((NY, *kept), i16),
        vmem((NY, *top), F32),
        vmem((snaps, RANK), F32),
        dma(3), dma(GROUPS), dma(GROUPS),
        dma(NZ), dma(NZ), dma(NZ), dma(NZ),
    ]
    return pl.pallas_call(
        kernel,
        out_shape=(jax.ShapeDtypeStruct((snaps, RANK), F32), jax.ShapeDtypeStruct(piece, F32)),
        in_specs=[pl.BlockSpec(memory_space=pltpu.HBM)] * 2,
        out_specs=(pl.BlockSpec(memory_space=pltpu.VMEM), pl.BlockSpec(memory_space=pltpu.VMEM)),
        scratch_shapes=scratch,
        compiler_params=pltpu.CompilerParams(collective_id=0, has_side_effects=True, vmem_limit_bytes=52 << 20),
    )(sketch_code.reshape(1, cols), anomalies)


def solution(mesh):
    return jax.shard_map(
        per_device,
        mesh=mesh,
        in_specs=(P("snap", "col"), P("col")),
        out_specs=(P("snap", None), P(("col", "snap"), None)),
        check_vma=False,
    )
```

```python
import functools

import jax
import jax.numpy as jnp
from jax import lax
from jax.experimental import pallas as pl
from jax.experimental.pallas import tpu as pltpu
from jax.sharding import PartitionSpec as P

RANK = 128
NX, NY, NZ, NC = 4, 4, 16, 2
NCOL = NY * NC
PLANE = NX * NCOL
ROWS = 64
TILE = NX * ROWS
LAG = 6
GROUP = 4
PANEL = 32
AHEAD = 8
F32 = jnp.float32
HIGHEST = lax.Precision.HIGHEST
MESH = pl.DeviceIdType.MESH
DIRECT, RELAYS, NEAR = (1, 15, 8, 4, 12, 2), (4, 12, 8), (1, 15, 2)

(S_CORE, S_Y, S_Y_TOP, S_BACK, R_X, R_X_TOP, R_Z, R_Z_TOP, G_Z, G_Z_TOP, G_X, G_X_TOP,
 GRAM_PLANE, GRAM_Z, GRAM_BACK, P_CORE, P_Y, P_Y_TOP, P_BACK) = range(19)
GROUPS = 19


def encode(value):
    top = jnp.maximum(jnp.max(jnp.abs(value), axis=0, keepdims=True), 1e-30)
    code = jnp.round(value * (32767.0 / top)).astype(jnp.int32).astype(jnp.int16)
    return code, top


def decode(code, top):
    return code.astype(jnp.int32).astype(F32) * (top * (1.0 / 32767.0))


def z_offset(j):
    return NZ // 2 + (1 - 2 * (j % 2)) * ((j + 1) // 2)


def factor_panel(m_ref, p):
    at = pl.multiple_of(p * PANEL, PANEL)
    g, e = m_ref[pl.ds(at, PANEL), :RANK], m_ref[pl.ds(at, PANEL), RANK:]
    g = pltpu.roll(g, lax.rem(RANK - at, RANK), 1)
    sub = lax.broadcasted_iota(jnp.int32, (PANEL, RANK), 0)
    lane = lax.broadcasted_iota(jnp.int32, (PANEL, RANK), 1)
    scale = jnp.zeros((PANEL, RANK), F32)
    for j in range(0, PANEL, AHEAD):
        columns = [jnp.broadcast_to(g[:, j + k : j + k + 1], (PANEL, RANK)) for k in range(AHEAD)]
        for k in range(AHEAD):
            row = j + k
            pivot = columns[k][row : row + 1, :]
            scale = jnp.where(sub == row, lax.rsqrt(pivot), scale)
            factor = jnp.where(sub > row, columns[k] * (1.0 / pivot), 0.0)
            for later in range(k + 1, AHEAD):
                columns[later] -= factor * columns[later][row : row + 1, :]
            g -= factor * g[row : row + 1, :]
            e -= factor * e[row : row + 1, :]
    w, e = pltpu.roll(g * scale, at, 1), e * scale
    both = jnp.concatenate([w, e], axis=1)
    m_ref[pl.ds(at, PANEL), :] = both
    below = jnp.where(lane >= at + PANEL, w, 0.0)
    m_ref[...] -= lax.dot_general(below, both, (((0,), (0,)), ((), ())), precision=HIGHEST, preferred_element_type=F32)


def kernel(
    code_hbm, a_hbm, scores_ref, eofs_ref,
    code_ref, a, omega, half, core_in, y_code, y_top, sketch, sketch_t, tile,
    x_out, x_out_top, x_in, x_in_top, x_own,
    z_out, z_out_top, z_in, z_in_top, basis,
    all_code, all_top,
    gram_out, gram_in, gram_z, gram_all, system,
    split, proj, proj_half, proj_in, proj_code, proj_top, proj_all,
    load_sem, send, recv, x_sem, x_top_sem, gz_sem, gx_sem,
):
    snap, col = lax.axis_index("snap"), lax.axis_index("col")
    z, x = snap // NX, snap % NX
    y, core = col // NC, col % NC
    place = x * NCOL + col

    def at_z(off):
        return {"snap": lax.rem(z + off, NZ) * NX + x, "col": col}

    def at_x(d):
        return {"snap": z * NX + lax.rem(x + d, NX), "col": col}

    def at_y(d):
        return {"snap": snap, "col": lax.rem(y + d, NY) * NC + core}

    def at_plane(e):
        other = lax.rem(place + e, PLANE)
        return {"snap": z * NX + other // NCOL, "col": other % NCOL}

    other_core = {"snap": snap, "col": y * NC + (1 - core)}

    def remote(src, dst, group, device, recv_sem=None):
        return pltpu.make_async_remote_copy(
            src_ref=src,
            dst_ref=dst,
            send_sem=send.at[group],
            recv_sem=recv.at[group] if recv_sem is None else recv_sem,
            device_id=device,
            device_id_type=MESH,
        )

    def wait_recv(region, group, recv_sem=None):
        remote(region, region, group, other_core, recv_sem).wait_recv()

    def wait_send(region, group):
        remote(region, region, group, other_core).wait_send()

    barrier = pltpu.get_barrier_semaphore()

    snaps = a.shape[0]
    kept = snaps // NC
    other_rows = pl.ds(pl.multiple_of((1 - core) * kept, kept), kept)
    core_rows = pl.ds(pl.multiple_of(core * kept, kept), kept)
    loads = [pltpu.make_async_copy(code_hbm, code_ref, load_sem.at[0])]
    loads += [pltpu.make_async_copy(a_hbm.at[r], a.at[r], load_sem.at[1 + i]) for i, r in enumerate((other_rows, core_rows))]
    for load in loads:
        load.start()

    @pl.loop(1, PLANE)
    def _(e):
        pl.semaphore_signal(barrier, inc=1, device_id=at_plane(e), device_id_type=MESH)

    @pl.loop(1, NZ)
    def _(d):
        pl.semaphore_signal(barrier, inc=1, device_id=at_z(d), device_id_type=MESH)

    width = 512
    loads[0].wait()

    @pl.loop(0, omega.shape[1] // width)
    def _(i):
        at = pl.ds(pl.multiple_of(i * width, width), width)
        code = code_ref[:, at]
        hits = lax.broadcasted_iota(jnp.int32, (RANK, width), 0) == code % RANK
        omega[:, at] = jnp.where(hits, jnp.where(code >= RANK, -1.0, 1.0), 0.0).astype(jnp.bfloat16)

    def sketch_rows(r):
        return lax.dot_general(a[r], omega[...], (((1,), (1,)), ((), ())), preferred_element_type=F32)

    loads[1].wait()
    half[...] = sketch_rows(other_rows)
    pl.semaphore_wait(barrier, PLANE - 1 + NZ - 1)
    to_core = remote(half, core_in, S_CORE, other_core)
    to_core.start()
    loads[2].wait()
    mine = sketch_rows(core_rows)

    def sum_over_y(value, code_buffer, top_buffer, group):
        code_buffer[y], top_buffer[y] = encode(value)
        for d in range(1, NY):
            remote(code_buffer.at[y], code_buffer.at[y], group, at_y(d)).start()
            remote(top_buffer.at[y], top_buffer.at[y], group + 1, at_y(d)).start()

    def summed_over_y(code_buffer, top_buffer, group):
        for k, buffer in enumerate((code_buffer, top_buffer)):
            wait_recv(buffer.at[pl.ds(0, NY - 1)], group + k)
            wait_send(buffer.at[pl.ds(0, NY - 1)], group + k)
        return sum(decode(code_buffer[i], top_buffer[i]) for i in range(NY))

    to_core.wait_recv()
    sum_over_y(mine + core_in[...], y_code, y_top, S_Y)
    to_core.wait_send()
    sketch[core_rows, :] = summed_over_y(y_code, y_top, S_Y).astype(jnp.bfloat16)
    remote(sketch.at[core_rows], sketch.at[core_rows], S_BACK, other_core).start()
    wait_recv(sketch.at[other_rows], S_BACK)
    sketch_t[...] = sketch[...].astype(F32).T.astype(jnp.bfloat16)
    wait_send(sketch.at[core_rows], S_BACK)

    def z_copies(j):
        return (
            remote(z_out.at[j], z_in.at[j], R_Z, at_z(z_offset(j))),
            remote(z_out_top.at[j], z_in_top.at[j], R_Z_TOP, at_z(z_offset(j))),
        )

    def tile_at(owner):
        return pl.ds(pl.multiple_of(owner * TILE, TILE), TILE)

    def produce(j):
        owner = lax.rem(z + z_offset(j), NZ)
        tile[...] = jnp.dot(sketch_t[...], a[:, tile_at(owner)], preferred_element_type=F32).T
        for d in range(1, NX):
            rows = pl.ds(pl.multiple_of(lax.rem(x + d, NX) * ROWS, ROWS), ROWS)
            x_out[j, d - 1], x_out_top[j, d - 1] = encode(tile[rows, :])
            remote(x_out.at[j, d - 1], x_in.at[j, d - 1], R_X, at_x(d), x_sem.at[j]).start()
            remote(x_out_top.at[j, d - 1], x_in_top.at[j, d - 1], R_X_TOP, at_x(d), x_top_sem.at[j]).start()
        x_own[j] = tile[pl.ds(pl.multiple_of(x * ROWS, ROWS), ROWS), :]

    def x_sum(j):
        wait_recv(x_in.at[j], R_X, x_sem.at[j])
        wait_recv(x_in_top.at[j], R_X_TOP, x_top_sem.at[j])
        total = x_own[j]
        for d in range(1, NX):
            total += decode(x_in[j, d - 1], x_in_top[j, d - 1])
        return total

    def consume(j):
        z_out[j], z_out_top[j] = encode(x_sum(j))
        for copy in z_copies(j):
            copy.start()

    pl.loop(0, LAG)(produce)

    @pl.loop(LAG, NZ)
    def _(j):
        produce(j)
        consume(j - LAG)

    pl.loop(NZ - LAG, NZ - 1)(consume)
    basis[...] = x_sum(NZ - 1)
    wait_recv(z_in, R_Z)
    wait_recv(z_in_top, R_Z_TOP)

    total = basis[...]
    for j in range(NZ - 1):
        total += decode(z_in[j], z_in_top[j])
    basis[...] = total

    own = basis[...]
    all_code[z, x], all_top[x, z] = encode(own)

    def gather_z(offset, d):
        owner = lax.rem(z - offset + NZ, NZ)
        chunk = all_code.at[owner, x]
        step = 2 + (NZ - 4) * lax.rem(owner, 2) if d == 2 else d
        remote(chunk, chunk, G_Z, at_z(step), gz_sem.at[lax.rem(offset + step, NZ)]).start()

    def gather_x(offset):
        chunk = all_code.at[lax.rem(z - offset + NZ, NZ), x]
        for d in range(1, NX):
            remote(chunk, chunk, G_X, at_x(d), gx_sem.at[offset]).start()

    def arrived(offset):
        wait_recv(all_code.at[lax.rem(z - offset + NZ, NZ), x], G_Z, gz_sem.at[offset])

    for d in DIRECT[:5]:
        gather_z(0, d)

    gram = lax.dot_general(own, own, (((0,), (0,)), ((), ())), precision=HIGHEST, preferred_element_type=F32)
    share = RANK // PLANE
    for i in range(PLANE):
        gram_out[i] = gram[i * share : (i + 1) * share, :]

    @pl.loop(1, PLANE)
    def _(e):
        remote(gram_out.at[lax.rem(place + e, PLANE)], gram_in.at[e - 1], GRAM_PLANE, at_plane(e)).start()

    for d in DIRECT[5:]:
        gather_z(0, d)

    @pl.loop(1, NZ)
    def _(d):
        remote(all_top.at[x, z], all_top.at[x, z], G_Z_TOP, at_z(d)).start()

    gather_x(0)

    for offset in (1, 15):
        arrived(offset)
        gather_x(offset)

    def relay(offset):
        arrived(offset)
        for d in NEAR:
            gather_z(offset, d)
        gather_x(offset)

    for offset in RELAYS[:2]:
        relay(offset)

    wait_recv(gram_in, GRAM_PLANE)
    gram_z[z] = gram_out[place] + jnp.sum(gram_in[...], axis=0)

    @pl.loop(1, NZ)
    def _(d):
        remote(gram_z.at[z], gram_z.at[z], GRAM_Z, at_z(d)).start()

    for offset in RELAYS[2:]:
        relay(offset)
    for offset in (2, 3, 5, 13, 11):
        arrived(offset)
        gather_x(offset)
    wait_recv(all_top.at[0, pl.ds(0, NZ - 1)], G_Z_TOP)
    for d in range(1, NX):
        remote(all_top.at[x], all_top.at[x], G_X_TOP, at_x(d)).start()
    for offset in (6, 14, 7, 9, 10):
        arrived(offset)
        gather_x(offset)

    wait_recv(gram_z.at[pl.ds(0, NZ - 1)], GRAM_Z)
    gram_all[place] = jnp.sum(gram_z[...], axis=0)

    @pl.loop(1, PLANE)
    def _(e):
        remote(gram_all.at[place], gram_all.at[place], GRAM_BACK, at_plane(e)).start()

    proj[...] = jnp.zeros_like(proj)
    wait_recv(all_top.at[pl.ds(0, NX - 1)], G_X_TOP)

    @pl.loop(0, NZ // GROUP)
    def _(i):
        first = lax.rem(z // GROUP + i, NZ // GROUP) * GROUP

        @pl.loop(0, GROUP)
        def _(t):
            owner = first + t
            wait_recv(all_code.at[owner, pl.ds(0, NX - 1)], G_X, gx_sem.at[lax.rem(z - owner + NZ, NZ)])
            for s in range(NX):
                value = decode(all_code[owner, s], all_top[s, owner])
                high = value.astype(jnp.bfloat16)
                rows = pl.ds(pl.multiple_of((t * NX + s) * ROWS, ROWS), ROWS)
                split[rows, :RANK] = high
                split[rows, RANK:] = (value - high.astype(F32)).astype(jnp.bfloat16)

        columns = pl.ds(pl.multiple_of(first * TILE, GROUP * TILE), GROUP * TILE)
        proj[...] += jnp.dot(a[:, columns], split[...], preferred_element_type=F32)

    proj_half[...] = proj[other_rows, :RANK] + proj[other_rows, RANK:]
    remote(proj_half, proj_in, P_CORE, other_core).start()
    mine = proj[core_rows, :RANK] + proj[core_rows, RANK:]
    wait_recv(proj_in, P_CORE)
    sum_over_y(mine + proj_in[...], proj_code, proj_top, P_Y)

    wait_recv(gram_all.at[pl.ds(0, PLANE - 1)], GRAM_BACK)
    for i in range(PLANE):
        system[i * share : (i + 1) * share, :RANK] = gram_all[i]
    square = (RANK, RANK)
    system[:, RANK:] = jnp.where(
        lax.broadcasted_iota(jnp.int32, square, 0) == lax.broadcasted_iota(jnp.int32, square, 1), 1.0, 0.0
    )
    pl.loop(0, RANK // PANEL)(functools.partial(factor_panel, system))

    proj_all[core_rows, :] = summed_over_y(proj_code, proj_top, P_Y)
    remote(proj_all.at[core_rows], proj_all.at[core_rows], P_BACK, other_core).start()

    def whiten(value):
        return lax.dot_general(
            value, system[:, RANK:], (((1,), (1,)), ((), ())), precision=HIGHEST, preferred_element_type=F32
        )

    scores_ref[core_rows, :] = whiten(proj_all[core_rows, :])
    eofs_ref[...] = whiten(basis[...])
    wait_recv(proj_all.at[other_rows], P_BACK)
    scores_ref[other_rows, :] = whiten(proj_all[other_rows, :])

    wait_send(x_out, R_X)
    wait_send(x_out_top, R_X_TOP)
    wait_send(z_out, R_Z)
    wait_send(z_out_top, R_Z_TOP)
    wait_send(z_in, G_Z)
    wait_send(x_in, G_X)
    wait_send(z_in_top, G_Z_TOP)
    wait_send(all_top.at[pl.ds(0, NX - 1)], G_X_TOP)
    wait_send(gram_in, GRAM_PLANE)
    wait_send(gram_z.at[pl.ds(0, NZ - 1)], GRAM_Z)
    wait_send(gram_in, GRAM_BACK)
    wait_send(proj_half, P_CORE)
    wait_send(proj_all.at[core_rows], P_BACK)


def per_device(anomalies, sketch_code):
    snaps, cols = anomalies.shape
    vmem, dma = pltpu.VMEM, lambda *shape: pltpu.SemaphoreType.DMA(shape)
    i16, bf16 = jnp.int16, jnp.bfloat16
    piece, top = (ROWS, RANK), (1, RANK)
    share = (RANK // PLANE, RANK)
    kept = (snaps // NC, RANK)
    scratch = [
        vmem((1, cols), jnp.int32),
        vmem((snaps, cols), bf16),
        vmem((RANK, cols), bf16),
        vmem(kept, F32),
        vmem(kept, F32),
        vmem((NY, *kept), i16),
        vmem((NY, *top), F32),
        vmem((snaps, RANK), bf16),
        vmem((RANK, snaps), bf16),
        vmem((TILE, RANK), F32),
        vmem((NZ, NX - 1, *piece), i16),
        vmem((NZ, NX - 1, *top), F32),
        vmem((NZ, NX - 1, *piece), i16),
        vmem((NZ, NX - 1, *top), F32),
        vmem((NZ, *piece), F32),
        vmem((NZ - 1, *piece), i16),
        vmem((NZ - 1, *top), F32),
        vmem((NZ - 1, *piece), i16),
        vmem((NZ - 1, *top), F32),
        vmem(piece, F32),
        vmem((NZ, NX, *piece), i16),
        vmem((NX, NZ, *top), F32),
        vmem((PLANE, *share), F32),
        vmem((PLANE - 1, *share), F32),
        vmem((NZ, *share), F32),
        vmem((PLANE, *share), F32),
        vmem((RANK, 2 * RANK), F32),
        vmem((GROUP * TILE, 2 * RANK), bf16),
        vmem((snaps, 2 * RANK), F32),
        vmem(kept, F32),
        vmem(kept, F32),
        vmem((NY, *kept), i16),
        vmem((NY, *top), F32),
        vmem((snaps, RANK), F32),
        dma(3), dma(GROUPS), dma(GROUPS),
        dma(NZ), dma(NZ), dma(NZ), dma(NZ),
    ]
    return pl.pallas_call(
        kernel,
        out_shape=(jax.ShapeDtypeStruct((snaps, RANK), F32), jax.ShapeDtypeStruct(piece, F32)),
        in_specs=[pl.BlockSpec(memory_space=pltpu.HBM)] * 2,
        out_specs=(pl.BlockSpec(memory_space=pltpu.VMEM), pl.BlockSpec(memory_space=pltpu.VMEM)),
        scratch_shapes=scratch,
        compiler_params=pltpu.CompilerParams(collective_id=0, has_side_effects=True, vmem_limit_bytes=52 << 20),
    )(sketch_code.reshape(1, cols), anomalies)


def solution(mesh):
    return jax.shard_map(
        per_device,
        mesh=mesh,
        in_specs=(P("snap", "col"), P("col")),
        out_specs=(P("snap", None), P(("col", "snap"), None)),
        check_vma=False,
    )
```
